32 devices in a mesh: dp: 4 (over y, x), tm: 4 (over z), height: 2 (over core).
Axes of the slice: x: 2, y: 2, z: 4, core: 2. Of those that a mesh axis runs over, the one named last changes fastest.
Arguments:
- video: bfloat16 [4, 8, 8, 64, 256], P('dp', 'tm', 'height'), may hold values from -6 to 6
- lengths: int32 [4], P('dp'), may hold values from 1 to 8
- enc_weight: bfloat16 [3, 3, 3, 256, 256], replicated, may hold values from -0.078125 to 0.078125
- dec_weight: bfloat16 [3, 3, 3, 256, 256], replicated, may hold values from -0.078125 to 0.078125
- cotangent: bfloat16 [4, 8, 8, 64, 256], P('dp', 'tm', 'height'), may hold values from -6 to 6
Outputs:
- output: bfloat16 [4, 8, 8, 64, 256], P('dp', 'tm', 'height')
- enc_grad: float32 [3, 3, 3, 256, 256], replicated
- dec_grad: float32 [3, 3, 3, 256, 256], replicated
The draws below stay inside these ranges and needn't reach their ends.
All inputs are finite; a program needn't handle non-finite values.
Results may differ from the reference program's by a relative error of at most 0.0045.
Values may be sent and summed in bfloat16 or wider, within the bound.
A program may use at most 128 MiB of HBM per device.

```python
import jax
import jax.numpy as jnp
from jax import lax

C = 256
COLS = 64
CLIPS = 4
FRAMES = 8
ROWS = 8


def set_ends(drawn, own_key, low, high):
    place = [jax.random.randint(jax.random.fold_in(own_key, axis), (), 0, length) for axis, length in enumerate(drawn.shape)]
    longest = drawn.shape.index(max(drawn.shape))
    beside = place[:longest] + [(place[longest] + 1) % drawn.shape[longest]] + place[longest + 1:]
    return drawn.at[tuple(place)].set(low).at[tuple(beside)].set(high)


def shard_levels(rng, extent, shards, smallest, largest):
    def one(axis_at, shards_of):
        draws = jax.random.uniform(jax.random.fold_in(jax.random.fold_in(rng, 6), axis_at), (shards_of,), jnp.float32, smallest / len(shards), largest / len(shards))
        return jnp.repeat(jnp.exp(draws), extent[axis_at] // shards_of).reshape((-1,) + (1,) * (len(extent) - axis_at - 1))

    gain = one(*shards[0])
    for cut in shards[1:]:
        gain = gain * one(*cut)
    return gain


def gaussian(key, extent, spread, reach, split=(), kind=jnp.bfloat16):
    array = spread * jax.random.normal(key, extent, jnp.float32)
    if split:
        array = array * shard_levels(key, extent, split, -0.22, 0.18)
    return jnp.clip(array, -reach, reach).astype(kind)


def setup_inputs(seed: int = 0) -> dict:
    seeds = jax.random.split(jax.random.key(seed), 6)
    return {
        "video": gaussian(seeds[0], (CLIPS, FRAMES, ROWS, COLS, C), 1.0, 6.0, ((0, 4), (1, 4), (2, 2))),
        "lengths": set_ends(jax.random.randint(seeds[1], (CLIPS,), 1, FRAMES + 1), jax.random.fold_in(seeds[1], 1), 1, FRAMES).astype(jnp.int32),
        "enc_weight": gaussian(seeds[2], (3, 3, 3, C, C), (27 * C) ** -0.5, 0.078125),
        "dec_weight": gaussian(seeds[3], (3, 3, 3, C, C), (27 * C) ** -0.5, 0.078125),
        "cotangent": gaussian(seeds[4], (CLIPS, FRAMES, ROWS, COLS, C), 1.0, 6.0, ((0, 4), (1, 4), (2, 2))),
    }


def apply_taps(ext, weight):
    count, frame_pad, row_pad, wide, chans = ext.shape
    frames = frame_pad - 2
    rows = row_pad - 2
    outs = weight.shape[-1]
    padded = jnp.pad(ext, ((0, 0), (0, 0), (0, 0), (1, 1), (0, 0)))
    stacked = jnp.concatenate([padded[:, :, :, e:e + wide, :] for e in range(3)], axis=-1)
    total = jnp.zeros((count * frames * rows * wide, outs), jnp.float32)
    for a in range(3):
        for b in range(3):
            slab = stacked[:, a:a + frames, b:b + rows].reshape(-1, 3 * chans)
            total = total + jnp.dot(slab, weight[a, b].reshape(3 * chans, outs), preferred_element_type=jnp.float32)
    return total.reshape(count, frames, rows, wide, outs)


def tap_grads(ext, cot):
    count, frame_pad, row_pad, wide, chans = ext.shape
    frames = frame_pad - 2
    rows = row_pad - 2
    outs = cot.shape[-1]
    padded = jnp.pad(ext, ((0, 0), (0, 0), (0, 0), (1, 1), (0, 0)))
    stacked = jnp.concatenate([padded[:, :, :, e:e + wide, :] for e in range(3)], axis=-1)
    flat = cot.reshape(-1, outs)
    result = []
    for a in range(3):
        for b in range(3):
            slab = stacked[:, a:a + frames, b:b + rows].reshape(-1, 3 * chans)
            result.append(lax.dot_general(slab, flat, (((0,), (0,)), ((), ())), preferred_element_type=jnp.float32))
    return jnp.stack(result).reshape(3, 3, 3, chans, outs)


def dsilu(value):
    sig = jax.nn.sigmoid(value)
    return sig * (1.0 + value * (1.0 - sig))


def reference(video, lengths, enc_weight, dec_weight, cotangent):
    flipped = jnp.transpose(dec_weight[::-1, ::-1, ::-1], (0, 1, 2, 4, 3))

    def one_clip(items):
        frames_in, cot, length = items
        tpos = jnp.arange(FRAMES, dtype=jnp.int32)
        keep = (tpos < length)[:, None, None, None]
        masked = jnp.where(keep, frames_in, jnp.zeros_like(frames_in))[None]
        cot_masked = jnp.where(keep, cot, jnp.zeros_like(cot))[None]
        ext_x = jnp.pad(masked, ((0, 0), (2, 0), (1, 1), (0, 0), (0, 0)))
        pre = apply_taps(ext_x, enc_weight)
        hidden = jax.nn.silu(pre).astype(jnp.bfloat16)
        ext_h = jnp.pad(hidden, ((0, 0), (2, 0), (1, 1), (0, 0), (0, 0)))
        output = (apply_taps(ext_h, dec_weight) + masked.astype(jnp.float32)).astype(jnp.bfloat16)
        ext_g = jnp.pad(cot_masked, ((0, 0), (0, 2), (1, 1), (0, 0), (0, 0)))
        back = apply_taps(ext_g, flipped)
        dpre = (back * dsilu(pre)).astype(jnp.bfloat16)
        return output[0], tap_grads(ext_x, dpre), tap_grads(ext_h, cot_masked)

    output, enc_parts, dec_parts = lax.map(one_clip, (video, cotangent, lengths.astype(jnp.int32)))
    return output, jnp.sum(enc_parts, axis=0), jnp.sum(dec_parts, axis=0)
```

```python
import jax
import jax.numpy as jnp
from jax import lax
from jax.sharding import PartitionSpec as P


def extended(shard, sides, width):
    for axis, dim in sides:
        devices, length = (lax.axis_size(axis), shard.shape[dim])
        up = [(i, (i + 1) % devices) for i in range(devices - 1)]
        down = [(j, i) for i, j in up]
        last = lax.slice_in_dim(shard, length - width, length, axis=dim)
        leading = lax.slice_in_dim(shard, 0, width, axis=dim)
        before = lax.ppermute(last, axis, up)
        after = lax.ppermute(leading, axis, down)
        shard = jnp.concatenate([before, shard, after], axis=dim)
    return shard


def from_behind(block, axis, distance):
    devices = range(lax.axis_size(axis))
    route = [(i - distance, i) for i in devices if i - distance in devices]
    return lax.ppermute(block, axis, route)


def apply_taps(ext, weight):
    count, frame_pad, row_pad, wide, chans = ext.shape
    frames = frame_pad - 2
    rows = row_pad - 2
    outs = weight.shape[-1]
    padded = jnp.pad(ext, ((0, 0), (0, 0), (0, 0), (1, 1), (0, 0)))
    stacked = jnp.concatenate([padded[:, :, :, e : e + wide, :] for e in range(3)], axis=-1)
    total = jnp.zeros((count * frames * rows * wide, outs), jnp.float32)
    for a in range(3):
        for b in range(3):
            slab = stacked[:, a : a + frames, b : b + rows].reshape(-1, 3 * chans)
            total = total + jnp.dot(
                slab, weight[a, b].reshape(3 * chans, outs), preferred_element_type=jnp.float32
            )
    return total.reshape(count, frames, rows, wide, outs)


def tap_grads(ext, cot):
    count, frame_pad, row_pad, wide, chans = ext.shape
    frames = frame_pad - 2
    rows = row_pad - 2
    outs = cot.shape[-1]
    padded = jnp.pad(ext, ((0, 0), (0, 0), (0, 0), (1, 1), (0, 0)))
    stacked = jnp.concatenate([padded[:, :, :, e : e + wide, :] for e in range(3)], axis=-1)
    flat = cot.reshape(-1, outs)
    result = []
    for a in range(3):
        for b in range(3):
            slab = stacked[:, a : a + frames, b : b + rows].reshape(-1, 3 * chans)
            result.append(
                lax.dot_general(
                    slab, flat, (((0,), (0,)), ((), ())), preferred_element_type=jnp.float32
                )
            )
    return jnp.stack(result).reshape(3, 3, 3, chans, outs)


def dsilu(value):
    sig = jax.nn.sigmoid(value)
    return sig * (1.0 + value * (1.0 - sig))


def row_edges(block):
    return extended(block, (("height", 2),), 1)


def with_earlier(block):
    before = from_behind(block, "tm", 1)
    return row_edges(jnp.concatenate([before, block], axis=1))


def with_later(block):
    after = from_behind(block, "tm", -1)
    return row_edges(jnp.concatenate([block, after], axis=1))


def index_bits(axis):
    size = lax.axis_size(axis)
    bits = []
    step = 1
    while step < size:
        bits.append((axis, step))
        step *= 2
    return bits


def swap(block, axis, step):
    return lax.ppermute(block, axis, [(i, i ^ step) for i in range(lax.axis_size(axis))])


def sum_part(part, order):
    trail = []
    for dim, (axis, step) in order:
        upper = lax.rem(lax.axis_index(axis) // step, 2) == 1
        low, high = jnp.split(part, 2, axis=dim)
        keep, give = jnp.where(upper, high, low), jnp.where(upper, low, high)
        got = swap(give.astype(jnp.bfloat16), axis, step)
        part = keep + got.astype(jnp.float32)
        trail.append((dim, axis, step, upper))
    part = part.astype(jnp.bfloat16)
    for dim, axis, step, upper in trail[::-1]:
        got = swap(part, axis, step)
        part = jnp.concatenate([jnp.where(upper, got, part), jnp.where(upper, part, got)], axis=dim)
    return part.astype(jnp.float32)


def sum_all(grad):
    height, dp, tm = index_bits("height"), index_bits("dp"), index_bits("tm")
    rest = height[1:]
    flat = grad.reshape(27, -1, grad.shape[-1])
    sums = []
    at = 0
    for count, order in ((10, dp + tm + rest), (10, dp[::-1] + tm + rest), (7, tm + dp + rest)):
        part = flat[at : at + count]
        at += count
        sums.append(sum_part(part, [(2, height[0])] + [(1, bit) for bit in order]))
    return jnp.concatenate(sums, axis=0).reshape(grad.shape)


def shards(video, lengths, enc_weight, dec_weight, cotangent):
    frames = video.shape[1]
    first_frame = lax.axis_index("tm") * frames
    tpos = first_frame + jnp.arange(frames, dtype=jnp.int32)
    keep = (tpos[None, :] < lengths[:, None])[:, :, None, None, None]
    masked = jnp.where(keep, video, jnp.zeros_like(video))
    cot_masked = jnp.where(keep, cotangent, jnp.zeros_like(cotangent))
    ext_x = with_earlier(masked)
    pre = apply_taps(ext_x, enc_weight)
    hidden = jax.nn.silu(pre).astype(jnp.bfloat16)
    ext_h = with_earlier(hidden)
    output = (apply_taps(ext_h, dec_weight) + masked.astype(jnp.float32)).astype(jnp.bfloat16)
    ext_g = with_later(cot_masked)
    flipped = jnp.transpose(dec_weight[::-1, ::-1, ::-1], (0, 1, 2, 4, 3))
    dec_local = tap_grads(ext_h, cot_masked)
    back = apply_taps(ext_g, flipped)
    dpre = (back * dsilu(pre)).astype(jnp.bfloat16)
    enc_local = tap_grads(ext_x, dpre)
    enc_grad, dec_grad = sum_all(enc_local), sum_all(dec_local)
    return (output, enc_grad, dec_grad)


def solution(mesh):
    in_specs = (
        P("dp", "tm", "height", None, None),
        P("dp"),
        P(),
        P(),
        P("dp", "tm", "height", None, None),
    )
    out_specs = (P("dp", "tm", "height", None, None), P(), P())
    return jax.shard_map(shards, mesh=mesh, in_specs=in_specs, out_specs=out_specs, check_vma=False)
```

```python
import jax
import jax.numpy as jnp
from jax import lax
from jax.sharding import PartitionSpec as P


def extended(shard, sides, width):
    for axis, dim in sides:
        devices, length = (lax.axis_size(axis), shard.shape[dim])
        up = [(i, (i + 1) % devices) for i in range(devices - 1)]
        down = [(j, i) for i, j in up]
        last = lax.slice_in_dim(shard, length - width, length, axis=dim)
        leading = lax.slice_in_dim(shard, 0, width, axis=dim)
        before = lax.ppermute(last, axis, up)
        after = lax.ppermute(leading, axis, down)
        shard = jnp.concatenate([before, shard, after], axis=dim)
    return shard


def from_behind(block, axis, distance):
    devices = range(lax.axis_size(axis))
    route = [(i - distance, i) for i in devices if i - distance in devices]
    return lax.ppermute(block, axis, route)


def apply_taps(ext, weight, transposed=False):
    count, frame_pad, row_pad, wide, chans = ext.shape
    frames = frame_pad - 2
    rows = row_pad - 2
    outs = weight.shape[2] if transposed else weight.shape[-1]
    padded = jnp.pad(ext, ((0, 0), (0, 0), (0, 0), (1, 1), (0, 0)))
    stacked = jnp.concatenate([padded[:, :, :, e : e + wide, :] for e in range(3)], axis=-1)
    total = jnp.zeros((count * frames * rows * wide, outs), jnp.float32)
    for a in range(3):
        for b in range(3):
            slab = stacked[:, a : a + frames, b : b + rows].reshape(-1, 3 * chans)
            if transposed:
                total = total + lax.dot_general(
                    slab, weight[a, b], (((1,), (1,)), ((), ())), preferred_element_type=jnp.float32
                )
                continue
            total = total + jnp.dot(
                slab, weight[a, b].reshape(3 * chans, outs), preferred_element_type=jnp.float32
            )
    return total.reshape(count, frames, rows, wide, outs)


def tap_grads(ext, cot):
    count, frame_pad, row_pad, wide, chans = ext.shape
    frames = frame_pad - 2
    rows = row_pad - 2
    outs = cot.shape[-1]
    padded = jnp.pad(ext, ((0, 0), (0, 0), (0, 0), (1, 1), (0, 0)))
    stacked = jnp.concatenate([padded[:, :, :, e : e + wide, :] for e in range(3)], axis=-1)
    flat = cot.reshape(-1, outs)
    result = []
    for a in range(3):
        for b in range(3):
            slab = stacked[:, a : a + frames, b : b + rows].reshape(-1, 3 * chans)
            result.append(
                lax.dot_general(
                    slab, flat, (((0,), (0,)), ((), ())), preferred_element_type=jnp.float32
                )
            )
    return jnp.stack(result).reshape(3, 3, 3, chans, outs)


def dsilu(value):
    sig = jax.nn.sigmoid(value)
    return sig * (1.0 + value * (1.0 - sig))


def row_edges(block):
    return extended(block, (("height", 2),), 1)


def with_earlier(block):
    before = from_behind(block, "tm", 1)
    return row_edges(jnp.concatenate([before, block], axis=1))


def with_later(block):
    after = from_behind(block, "tm", -1)
    return row_edges(jnp.concatenate([block, after], axis=1))


def index_bits(axis):
    size = lax.axis_size(axis)
    bits = []
    step = 1
    while step < size:
        bits.append((axis, step))
        step *= 2
    return bits


def swap(block, axis, step):
    return lax.ppermute(block, axis, [(i, i ^ step) for i in range(lax.axis_size(axis))])


def sum_part(part, order):
    trail = []
    for dim, (axis, step) in order:
        upper = lax.rem(lax.axis_index(axis) // step, 2) == 1
        low, high = jnp.split(part, 2, axis=dim)
        keep, give = jnp.where(upper, high, low), jnp.where(upper, low, high)
        got = swap(give.astype(jnp.bfloat16), axis, step)
        part = keep + got.astype(jnp.float32)
        trail.append((dim, axis, step, upper))
    part = part.astype(jnp.bfloat16)
    for dim, axis, step, upper in trail[::-1]:
        got = swap(part, axis, step)
        part = jnp.concatenate([jnp.where(upper, got, part), jnp.where(upper, part, got)], axis=dim)
    return part.astype(jnp.float32)


def sum_all(grad):
    height, dp, tm = index_bits("height"), index_bits("dp"), index_bits("tm")
    rest = height[1:]
    flat = grad.reshape(27, -1, grad.shape[-1])
    sums = []
    at = 0
    for count, order in ((10, dp + tm + rest), (10, dp[::-1] + tm + rest), (7, tm + dp + rest)):
        part = flat[at : at + count]
        at += count
        sums.append(sum_part(part, [(2, height[0])] + [(1, bit) for bit in order]))
    return jnp.concatenate(sums, axis=0).reshape(grad.shape)


def shards(video, lengths, enc_weight, dec_weight, cotangent):
    frames = video.shape[1]
    first_frame = lax.axis_index("tm") * frames
    tpos = first_frame + jnp.arange(frames, dtype=jnp.int32)
    keep = (tpos[None, :] < lengths[:, None])[:, :, None, None, None]
    masked = jnp.where(keep, video, jnp.zeros_like(video))
    cot_masked = jnp.where(keep, cotangent, jnp.zeros_like(cotangent))
    ext_x = with_earlier(masked)
    pre = apply_taps(ext_x, enc_weight)
    hidden = jax.nn.silu(pre).astype(jnp.bfloat16)
    ext_h = with_earlier(hidden)
    output = (apply_taps(ext_h, dec_weight) + masked.astype(jnp.float32)).astype(jnp.bfloat16)
    ext_g = with_later(cot_masked)
    chans = dec_weight.shape[3]
    flipped = jnp.transpose(dec_weight[::-1, ::-1, ::-1], (0, 1, 3, 2, 4)).reshape(3, 3, chans, -1)
    dec_local = tap_grads(ext_h, cot_masked)
    back = apply_taps(ext_g, flipped, True)
    dpre = (back * dsilu(pre)).astype(jnp.bfloat16)
    enc_local = tap_grads(ext_x, dpre)
    enc_grad, dec_grad = sum_all(enc_local), sum_all(dec_local)
    return (output, enc_grad, dec_grad)


def solution(mesh):
    in_specs = (
        P("dp", "tm", "height", None, None),
        P("dp"),
        P(),
        P(),
        P("dp", "tm", "height", None, None),
    )
    out_specs = (P("dp", "tm", "height", None, None), P(), P())
    return jax.shard_map(shards, mesh=mesh, in_specs=in_specs, out_specs=out_specs, check_vma=False)
```
